256 devices in a mesh: lat: 16 (over z_lo, x, core), src: 16 (over y, z_hi).
Axes of the slice: x: 4, y: 4, z: 8 (z_hi: 4, z_lo: 2; z = z_hi * 2 + z_lo), core: 2. Of those that a mesh axis runs over, the one named last changes fastest.
Arguments:
- fine_residual: bfloat16 [32, 32, 256, 2048], P('lat', 'src'), may hold values from -6 to 6
- basis: bfloat16 [32, 32, 2048, 128], P('lat', 'src'), may hold values from -0.25 to 0.25
- diag_inverse: bfloat16 [32, 32, 128, 128], P('lat', 'src'), may hold values from -0.32 to 1.7, as said below
- hoppings: bfloat16 [32, 32, 8, 128, 128], P('lat', 'src'), may hold values from -0.125 to 0.125
- neighbours: int32 [32, 6], replicated, may hold values from 0 to 31, as said below
- aggregation: int32 [32, 32], P('lat', 'src'), may hold values from 0 to 31, as said below
Outputs:
- correction: bfloat16 [32, 32, 256, 2048], P('lat', 'src')
The draws below stay inside these ranges and needn't reach their ends.
Inputs may be any that keep to these rules, and one draw needn't show every extreme that they name: `diag_inverse`: a site's diagonal inverse is one on the diagonal within a fifth (two fifths in some draws) plus independent off-diagonal entries. The spatial sites form a periodic grid of 16 by 1 by 2 sites, site (x, y, z) having index (x * 1 + y) * 2 + z; columns 2k and 2k+1 hold the two periodic neighbours along grid direction k, one step up and one step down, in an order drawn for each k. `aggregation`: in each row, every aligned block of 2 entries is a permutation of that block's own column indices.
All inputs are finite; a program needn't handle non-finite values.
Results may differ from the reference program's by a relative error of at most 0.0075.
Values may be sent and summed in bfloat16 or wider, within the bound.
No kernel may reach another device: no remote copies, remote signals or barrier semaphores. Data moves between devices by JAX's collectives and lax.ppermute only.
A program may use at most 128 MiB of HBM per device.

```python
import math
import jax
import jax.numpy as jnp
from jax import lax

FINE = 2048
CDOF = 128
NSRC = 256
SWEEPS = 3
SP_DEV = 2
NT = 32
SPACE = 32


def draw_diag_inverse(key, part):
    first_key, second_key = jax.random.split(key)
    identity = jnp.eye(CDOF, dtype=jnp.float32)
    off_diag = jnp.clip(jax.random.normal(first_key, (NT, SPACE, CDOF, CDOF), jnp.float32) * (0.5 / math.sqrt(CDOF)), -0.3, 0.3)
    diag_part = jax.random.uniform(second_key, (NT, SPACE, 1, 1), jnp.float32, 0.8, 1.2)
    return (off_diag * (1.0 - identity) + diag_part * identity).astype(jnp.bfloat16)


def grid_index(x_pos, y_pos, z_pos, y_len):
    return ((x_pos * y_len + y_pos) * 2 + z_pos).astype(jnp.int32)


def draw_neighbours(key, part):
    flips = jax.random.randint(jax.random.fold_in(key, 17), (3,), 0, 2).astype(jnp.int32)
    x_len = SPACE // SP_DEV
    y_len = SP_DEV // 2
    sites = jnp.arange(SPACE, dtype=jnp.int32)
    z_pos = sites % 2
    y_pos = sites // 2 % y_len
    x_pos = sites // SP_DEV
    pairs = [(grid_index((x_pos + 1) % x_len, y_pos, z_pos, y_len), grid_index((x_pos + x_len - 1) % x_len, y_pos, z_pos, y_len)), (grid_index(x_pos, (y_pos + 1) % y_len, z_pos, y_len), grid_index(x_pos, (y_pos + y_len - 1) % y_len, z_pos, y_len)), (grid_index(x_pos, y_pos, (z_pos + 1) % 2, y_len), grid_index(x_pos, y_pos, (z_pos + 1) % 2, y_len))]
    columns = []
    for direction in range(3):
        upward, downward = pairs[direction]
        flipped = flips[direction] == 1
        columns.append(jnp.where(flipped, downward, upward))
        columns.append(jnp.where(flipped, upward, downward))
    return jnp.stack(columns, axis=1).astype(jnp.int32)


def draw_aggregation(key, part):
    blocks = SPACE // SP_DEV
    subkeys = jax.random.split(key, NT * blocks)
    within = jax.vmap(lambda single: jax.random.permutation(single, SP_DEV))(subkeys).astype(jnp.int32)
    offsets = jnp.arange(NT * blocks, dtype=jnp.int32) % blocks * SP_DEV
    return (within + offsets[:, None]).reshape(NT, SPACE)


def block_scale(key, dims, shards, least, largest):
    gain = 1.0
    for axis_at, shards_of in shards:
        draws = jax.random.uniform(jax.random.fold_in(jax.random.fold_in(key, 6), axis_at), (shards_of,), jnp.float32, least / len(shards), largest / len(shards))
        gain = gain * jnp.repeat(jnp.exp(draws), dims[axis_at] // shards_of).reshape((-1,) + (1,) * (len(dims) - 1 - axis_at))
    return gain


def noise(key, dims, deviation, bound, cuts=(), held_as=jnp.bfloat16):
    entries = jax.random.normal(key, dims, jnp.float32) * deviation
    if len(cuts) > 0:
        entries = block_scale(key, dims, cuts, -0.22, 0.18) * entries
    return jnp.clip(entries, min=-bound, max=bound).astype(held_as)


def setup_inputs(seed: int = 0) -> dict:
    streams_of = jax.random.split(jax.random.key(seed), 7)
    return {
        "fine_residual": noise(streams_of[0], (NT, SPACE, NSRC, FINE), 1.0, 6.0, ((0, 16), (1, 16))),
        "basis": noise(streams_of[1], (NT, SPACE, FINE, CDOF), (FINE // 4) ** -0.5, 0.25, ((0, 16), (1, 16))),
        "diag_inverse": draw_diag_inverse(jax.random.fold_in(streams_of[6], 71), 0),
        "hoppings": noise(streams_of[3], (NT, SPACE, 8, CDOF, CDOF), (16 * CDOF) ** -0.5, 0.125, ((0, 16), (1, 16))),
        "neighbours": draw_neighbours(jax.random.fold_in(streams_of[6], 71), 0),
        "aggregation": draw_aggregation(jax.random.fold_in(streams_of[6], 71), 0),
    }


damping = 0.8


def hop_sum(iterate, hoppings, neighbours, slices):
    def per_slice(slice_index):
        current = iterate[slice_index]
        spatial = jnp.take(current, neighbours, axis=0)
        upper_time = iterate[(slice_index + 1) % NT]
        lower_time = iterate[(slice_index + NT - 1) % NT]
        stacked = jnp.concatenate([spatial, upper_time[:, None], lower_time[:, None]], axis=1).astype(jnp.float32)
        return jnp.einsum('sknc,skcd->snd', stacked, hoppings[slice_index].astype(jnp.float32))
    return lax.map(per_slice, slices)


def reference(fine_residual, basis, diag_inverse, hoppings, neighbours, aggregation):
    slices = jnp.arange(NT, dtype=jnp.int32)

    def restrict_slice(slice_index):
        return jnp.einsum('snr,src->snc', fine_residual[slice_index].astype(jnp.float32), basis[slice_index].astype(jnp.float32)).astype(jnp.bfloat16)

    restricted = lax.map(restrict_slice, slices)
    inverse = jnp.argsort(aggregation, axis=1).astype(jnp.int32)
    coarse_rhs = jnp.take_along_axis(restricted, inverse[:, :, None, None], axis=1)
    inverse_blocks = diag_inverse.astype(jnp.float32)
    applied = jnp.einsum('tsnc,tscd->tsnd', coarse_rhs.astype(jnp.float32), inverse_blocks)
    iterate = (damping * applied).astype(jnp.bfloat16)
    for sweep_index in range(SWEEPS - 1):
        hop_terms = hop_sum(iterate, hoppings, neighbours, slices)
        difference = (coarse_rhs.astype(jnp.float32) - hop_terms).astype(jnp.bfloat16)
        applied = jnp.einsum('tsnc,tscd->tsnd', difference.astype(jnp.float32), inverse_blocks)
        iterate = ((1.0 - damping) * iterate.astype(jnp.float32) + damping * applied).astype(jnp.bfloat16)
    gathered = jnp.take_along_axis(iterate, aggregation[:, :, None, None], axis=1)

    def prolong_slice(slice_index):
        return jnp.einsum('snc,src->snr', gathered[slice_index].astype(jnp.float32), basis[slice_index].astype(jnp.float32)).astype(jnp.bfloat16)

    return lax.map(prolong_slice, slices)
```

```python
import jax
import jax.numpy as jnp
from jax import lax
from jax.experimental import pallas as pl
from jax.experimental.pallas import tpu as pltpu
from jax.sharding import PartitionSpec as P

CHUNKS = 2
DAMPING = 0.8
KEEP = 1.0 - DAMPING
BF16 = jnp.bfloat16
F32 = jnp.float32


def dot(a, b):
    return jnp.dot(a, b, preferred_element_type=F32)


def params():
    return pltpu.CompilerParams(
        dimension_semantics=("arbitrary", "arbitrary"), vmem_limit_bytes=24 * 1024 * 1024
    )


def full(shape):
    return pl.BlockSpec(shape, lambda *_: (0,) * len(shape))


def put_iterate(t, c, value, whole, first, last):
    whole[t, c] = value

    @pl.when(t == 0)
    def _():
        first[c] = value

    @pl.when(t == whole.shape[0] - 1)
    def _():
        last[c] = value


def restrict_kernel(agg, fine, basis, dinv, rhs, e, first, last):
    t, s = pl.program_id(0), pl.program_id(1)
    c = agg[t, s] & 1
    r = dot(fine[0, 0], basis[0, 0]).astype(BF16)
    rhs[t, c] = r
    put_iterate(t, c, (DAMPING * dot(r, dinv[0, 0])).astype(BF16), e, first, last)


def restrict(j, n, agg, fine, basis, dinv):
    nt, ns, _, nf = fine.shape
    nc = basis.shape[3]
    whole = (nt, ns, n, nc)
    edge = (ns, n, nc)
    return pl.pallas_call(
        restrict_kernel,
        grid_spec=pltpu.PrefetchScalarGridSpec(
            num_scalar_prefetch=1,
            grid=(nt, ns),
            in_specs=[
                pl.BlockSpec((1, 1, n, nf), lambda t, s, a: (t, s, j, 0)),
                pl.BlockSpec((1, 1, nf, nc), lambda t, s, a: (t, s, 0, 0)),
                pl.BlockSpec((1, 1, nc, nc), lambda t, s, a: (t, a[t, s] & 1, 0, 0)),
            ],
            out_specs=[full(whole), full(whole), full(edge), full(edge)],
        ),
        out_shape=[
            jax.ShapeDtypeStruct(whole, BF16),
            jax.ShapeDtypeStruct(whole, BF16),
            jax.ShapeDtypeStruct(edge, BF16),
            jax.ShapeDtypeStruct(edge, BF16),
        ],
        compiler_params=params(),
        cost_estimate=pl.CostEstimate(
            flops=2 * nt * ns * n * nc * (nf + nc),
            bytes_accessed=2 * nt * ns * (n * nf + nf * nc),
            transcendentals=0,
        ),
        name="restrict",
    )(agg, fine, basis, dinv)


def next_iterate(agg, nbr, t, c, rhs, e, up, dn, lup, ldn, hops, dinv):
    nt = e.shape[0]
    site = (agg[0, 0] & -2) + c
    upward = nbr[site, 0] == (site + 2) % nbr.shape[0]
    own, other = e[t, c], e[t, 1 - c]
    above, below = up[0, 0], dn[0, 0]
    later = jnp.where(t == nt - 1, lup[c], e[jnp.minimum(t + 1, nt - 1), c])
    earlier = jnp.where(t == 0, ldn[c], e[jnp.maximum(t - 1, 0), c])
    stacked = jnp.concatenate(
        [
            jnp.where(upward, above, below),
            jnp.where(upward, below, above),
            own,
            own,
            other,
            other,
            later,
            earlier,
        ],
        axis=1,
    )
    nc = own.shape[1]
    hop = dot(stacked, hops[0, 0].reshape(8 * nc, nc))
    difference = (rhs[0, 0].astype(F32) - hop).astype(BF16)
    return (KEEP * own.astype(F32) + DAMPING * dot(difference, dinv[0, 0])).astype(BF16)


def sweep_kernel(agg, nbr, rhs, e, up, dn, lup, ldn, hops, dinv, out, first, last):
    t, c = pl.program_id(0), pl.program_id(1)
    value = next_iterate(agg, nbr, t, c, rhs, e, up, dn, lup, ldn, hops, dinv)
    put_iterate(t, c, value, out, first, last)


def sweep(agg, nbr, rhs, e, halo, hops, dinv):
    nt, ns, n, nc = e.shape
    edge = (ns, n, nc)
    block = pl.BlockSpec((1, 1, n, nc), lambda t, c, a, b: (t, c, 0, 0))
    return pl.pallas_call(
        sweep_kernel,
        grid_spec=pltpu.PrefetchScalarGridSpec(
            num_scalar_prefetch=2,
            grid=(nt, ns),
            in_specs=[
                block,
                full(e.shape),
                block,
                block,
                full(edge),
                full(edge),
                pl.BlockSpec((1, 1, 8, nc, nc), lambda t, c, a, b: (t, c, 0, 0, 0)),
                pl.BlockSpec((1, 1, nc, nc), lambda t, c, a, b: (t, c, 0, 0)),
            ],
            out_specs=[full(e.shape), full(edge), full(edge)],
        ),
        out_shape=[
            jax.ShapeDtypeStruct(e.shape, BF16),
            jax.ShapeDtypeStruct(edge, BF16),
            jax.ShapeDtypeStruct(edge, BF16),
        ],
        compiler_params=params(),
        cost_estimate=pl.CostEstimate(
            flops=2 * nt * ns * n * nc * 9 * nc,
            bytes_accessed=2 * nt * ns * (9 * nc * nc + 5 * n * nc),
            transcendentals=0,
        ),
        name="sweep",
    )(agg, nbr, rhs, e, *halo, hops, dinv)


def prolong_kernel(agg, nbr, rhs, e, up, dn, lup, ldn, hops, dinv, basis, *rest):
    out = rest[-1]
    t, s = pl.program_id(0), pl.program_id(1)
    c = agg[t, s] & 1
    value = next_iterate(agg, nbr, t, c, rhs, e, up, dn, lup, ldn, hops, dinv)
    out[0, 0] = lax.dot_general(
        value, basis[0, 0], (((1,), (1,)), ((), ())), preferred_element_type=F32
    ).astype(BF16)


def prolong(j, shape, agg, nbr, rhs, e, halo, hops, dinv, basis, previous):
    nt, ns, n, nc = e.shape
    nf = basis.shape[2]
    edge = (ns, n, nc)
    at_site = lambda t, s, a, b: (t, a[t, s] & 1, 0, 0)
    block = pl.BlockSpec((1, 1, n, nc), at_site)
    in_specs = [
        block,
        full(e.shape),
        block,
        block,
        full(edge),
        full(edge),
        pl.BlockSpec((1, 1, 8, nc, nc), lambda t, s, a, b: (t, a[t, s] & 1, 0, 0, 0)),
        pl.BlockSpec((1, 1, nc, nc), at_site),
        pl.BlockSpec((1, 1, nf, nc), lambda t, s, a, b: (t, s, 0, 0)),
    ]
    operands = [agg, nbr, rhs, e, *halo, hops, dinv, basis]
    aliases = {}
    if previous is not None:
        aliases = {len(operands): 0}
        in_specs.append(pl.BlockSpec(memory_space=pl.ANY))
        operands.append(previous)
    return pl.pallas_call(
        prolong_kernel,
        grid_spec=pltpu.PrefetchScalarGridSpec(
            num_scalar_prefetch=2,
            grid=(nt, ns),
            in_specs=in_specs,
            out_specs=pl.BlockSpec((1, 1, n, nf), lambda t, s, a, b: (t, s, j, 0)),
        ),
        out_shape=jax.ShapeDtypeStruct(shape, BF16),
        input_output_aliases=aliases,
        compiler_params=params(),
        cost_estimate=pl.CostEstimate(
            flops=2 * nt * ns * n * nc * (9 * nc + nf),
            bytes_accessed=2 * nt * ns * (9 * nc * nc + 5 * n * nc + nf * nc + n * nf),
            transcendentals=0,
        ),
        name="prolong",
    )(*operands)


def exchange(e, first, last):
    def from_next(x, axis):
        count = lax.axis_size(axis)
        return lax.ppermute(x, axis, [((i + 1) % count, i) for i in range(count)])

    def from_previous(x, axis):
        count = lax.axis_size(axis)
        return lax.ppermute(x, axis, [(i, (i + 1) % count) for i in range(count)])

    return (
        from_next(e, "src"),
        from_previous(e, "src"),
        from_next(first, "lat"),
        from_previous(last, "lat"),
    )


def body(fine, basis, dinv, hops, nbr, agg):
    n = fine.shape[2] // CHUNKS
    state = []
    for j in range(CHUNKS):
        rhs, e, first, last = restrict(j, n, agg, fine, basis, dinv)
        state.append((rhs, e, exchange(e, first, last)))
    for j in range(CHUNKS):
        rhs, e, halo = state[j]
        e, first, last = sweep(agg, nbr, rhs, e, halo, hops, dinv)
        state[j] = (rhs, e, exchange(e, first, last))
    out = None
    for j in range(CHUNKS):
        rhs, e, halo = state[j]
        out = prolong(j, fine.shape, agg, nbr, rhs, e, halo, hops, dinv, basis, out)
    return out


def solution(mesh):
    return jax.shard_map(
        body,
        mesh=mesh,
        in_specs=(
            P("lat", "src", None, None),
            P("lat", "src", None, None),
            P("lat", "src", None, None),
            P("lat", "src", None, None, None),
            P(),
            P("lat", "src"),
        ),
        out_specs=P("lat", "src", None, None),
        check_vma=False,
    )
```

```python
import functools

import jax
import jax.numpy as jnp
from jax import lax
from jax.experimental import pallas as pl
from jax.experimental.pallas import tpu as pltpu
from jax.sharding import PartitionSpec as P

DAMPING = 0.8
KEEP = 1.0 - DAMPING
BF16 = jnp.bfloat16
F32 = jnp.float32
PIECES = 4
HBM = pl.BlockSpec(memory_space=pltpu.HBM)
VMEM = pl.BlockSpec(memory_space=pltpu.VMEM)
PARAMS = pltpu.CompilerParams(vmem_limit_bytes=32 * 1024 * 1024)


def in_hbm(x):
    return pltpu.with_memory_space_constraint(x, pltpu.HBM)


def in_vmem(x):
    return pltpu.with_memory_space_constraint(x, pltpu.VMEM)


def dot(a, b):
    return jnp.dot(a, b, preferred_element_type=F32)


class Copies:
    def __init__(self, sems):
        self.sems = sems
        self.count = 0

    def start(self, src, dst):
        copy = pltpu.make_async_copy(src, dst, self.sems.at[self.count])
        self.count += 1
        copy.start()
        return copy


def restrict_kernel(
    t, agg, fine, basis, dinv, rhs, e, agg_s, fine_v, basis_v, dinv_v, sems
):
    ns, n = fine_v.shape[0], fine_v.shape[1]
    rows = n // PIECES
    copies = Copies(sems)
    agg_in = copies.start(agg, agg_s)
    basis_in, fine_in = [], []
    for s in range(ns):
        basis_in.append(copies.start(basis.at[t, s], basis_v.at[s]))
        for p in range(PIECES):
            part = pl.ds(p * rows, rows)
            fine_in.append(copies.start(fine.at[t, s, part], fine_v.at[s, part]))
    dinv_in = copies.start(dinv.at[t], dinv_v)
    agg_in.wait()
    for s in range(ns):
        c = agg_s[t, s] & 1
        basis_in[s].wait()
        if s == 0:
            dinv_in.wait()
        for p in range(PIECES):
            part = pl.ds(p * rows, rows)
            fine_in[s * PIECES + p].wait()
            r = dot(fine_v[s, part], basis_v[s]).astype(BF16)
            rhs[c, part] = r
            e[c, part] = (DAMPING * dot(r, dinv_v[c])).astype(BF16)


def restrict(t, agg, fine, basis, dinv):
    _, ns, n, nf = fine.shape
    nc = basis.shape[3]
    part = pltpu.VMEM((ns, n, nc), BF16)
    return pl.pallas_call(
        functools.partial(restrict_kernel, t),
        in_specs=[HBM] * 4,
        out_specs=[VMEM] * 2,
        out_shape=[part, part],
        scratch_shapes=[
            pltpu.SMEM(agg.shape, jnp.int32),
            pltpu.VMEM((ns, n, nf), BF16),
            pltpu.VMEM((ns, nf, nc), BF16),
            pltpu.VMEM((ns, nc, nc), BF16),
            pltpu.SemaphoreType.DMA((2 + ns * (PIECES + 1),)),
        ],
        compiler_params=PARAMS,
        cost_estimate=pl.CostEstimate(
            flops=2 * ns * n * nc * (nf + nc),
            bytes_accessed=2 * ns * (n * nf + nf * nc),
            transcendentals=0,
        ),
        name="restrict",
    )(*map(in_hbm, (agg, fine, basis, dinv)))


def next_iterate(c, upward, rhs, e, later, earlier, up, dn, hops, dinv):
    ns, _, nc = e.shape
    own, other = e[c], e[ns - 1 - c]
    above, below = up[c], dn[c]
    stacked = jnp.concatenate(
        [
            jnp.where(upward, above, below),
            jnp.where(upward, below, above),
            own,
            own,
            other,
            other,
            later[c],
            earlier[c],
        ],
        axis=1,
    )
    hop = dot(stacked, hops[c].reshape(8 * nc, nc))
    difference = (rhs[c].astype(F32) - hop).astype(BF16)
    return (KEEP * own.astype(F32) + DAMPING * dot(difference, dinv[c])).astype(BF16)


def is_upward(c, agg_s, nbr_s):
    spatial = nbr_s.shape[1]
    site = (agg_s[0, 0] & -2) + c
    return nbr_s[0, site] == lax.rem(site + 2, spatial)


def fetch_sweep(copies, t, agg, nbr, hops, dinv, agg_s, nbr_s, hops_v, dinv_v):
    return [
        copies.start(agg, agg_s),
        copies.start(nbr, nbr_s),
        copies.start(hops.at[t], hops_v),
        copies.start(dinv.at[t], dinv_v),
    ]


def sweep_kernel(t, *refs):
    agg, nbr = refs[:2]
    coarse = refs[2:8]
    hops, dinv, out, agg_s, nbr_s, hops_v, dinv_v, sems = refs[8:]
    for wait in fetch_sweep(
        Copies(sems), t, agg, nbr, hops, dinv, agg_s, nbr_s, hops_v, dinv_v
    ):
        wait.wait()
    for c in range(out.shape[0]):
        out[c] = next_iterate(c, is_upward(c, agg_s, nbr_s), *coarse, hops_v, dinv_v)


def sweep_scratch(agg, nbr, shape):
    ns, _, nc = shape
    return [
        pltpu.SMEM(agg.shape, jnp.int32),
        pltpu.SMEM(nbr.shape, jnp.int32),
        pltpu.VMEM((ns, 8, nc, nc), BF16),
        pltpu.VMEM((ns, nc, nc), BF16),
    ]


def sweep(t, agg, nbr, coarse, hops, dinv):
    shape = coarse[0].shape
    ns, n, nc = shape
    return pl.pallas_call(
        functools.partial(sweep_kernel, t),
        in_specs=[HBM] * 2 + [VMEM] * 6 + [HBM] * 2,
        out_specs=VMEM,
        out_shape=pltpu.VMEM(shape, BF16),
        scratch_shapes=[
            *sweep_scratch(agg, nbr, shape),
            pltpu.SemaphoreType.DMA((4,)),
        ],
        compiler_params=PARAMS,
        cost_estimate=pl.CostEstimate(
            flops=2 * ns * n * nc * 9 * nc,
            bytes_accessed=2 * ns * (9 * nc * nc + 7 * n * nc),
            transcendentals=0,
        ),
        name="sweep",
    )(in_hbm(agg), in_hbm(nbr), *map(in_vmem, coarse), in_hbm(hops), in_hbm(dinv))


def prolong_kernel(t, *refs):
    agg, nbr = refs[:2]
    coarse = refs[2:8]
    hops, dinv, basis = refs[8:11]
    out, agg_s, nbr_s, hops_v, dinv_v, basis_v, out_v, sems = refs[len(refs) - 8 :]
    ns, n, nf = out_v.shape
    rows = n // PIECES
    copies = Copies(sems)
    waits = fetch_sweep(copies, t, agg, nbr, hops, dinv, agg_s, nbr_s, hops_v, dinv_v)
    basis_in = [copies.start(basis.at[t, s], basis_v.at[s]) for s in range(ns)]
    for wait in waits:
        wait.wait()
    outs = []
    for s in range(ns):
        c = agg_s[t, s] & 1
        value = next_iterate(c, is_upward(c, agg_s, nbr_s), *coarse, hops_v, dinv_v)
        basis_in[s].wait()
        for p in range(PIECES):
            part = pl.ds(p * rows, rows)
            out_v[s, part] = lax.dot_general(
                value[p * rows : (p + 1) * rows],
                basis_v[s],
                (((1,), (1,)), ((), ())),
                preferred_element_type=F32,
            ).astype(BF16)
            outs.append(copies.start(out_v.at[s, part], out.at[t, s, part]))
    for wait in outs:
        wait.wait()


def prolong(t, shape, agg, nbr, coarse, hops, dinv, basis, previous):
    part = coarse[0].shape
    ns, n, nc = part
    nf = basis.shape[2]
    operands = [in_hbm(agg), in_hbm(nbr), *map(in_vmem, coarse)]
    operands += map(in_hbm, (hops, dinv, basis))
    in_specs = [HBM] * 2 + [VMEM] * 6 + [HBM] * 3
    aliases = {}
    if previous is not None:
        aliases = {len(operands): 0}
        operands.append(in_hbm(previous))
        in_specs.append(HBM)
    return pl.pallas_call(
        functools.partial(prolong_kernel, t),
        in_specs=in_specs,
        out_specs=HBM,
        out_shape=pltpu.HBM(shape, BF16),
        input_output_aliases=aliases,
        scratch_shapes=[
            *sweep_scratch(agg, nbr, part),
            pltpu.VMEM((ns, nf, nc), BF16),
            pltpu.VMEM((ns, n, nf), BF16),
            pltpu.SemaphoreType.DMA((4 + ns * (PIECES + 1),)),
        ],
        compiler_params=PARAMS,
        cost_estimate=pl.CostEstimate(
            flops=2 * ns * n * nc * (9 * nc + nf),
            bytes_accessed=2 * ns * (9 * nc * nc + 6 * n * nc + nf * nc + n * nf),
            transcendentals=0,
        ),
        name="prolong",
    )(*operands)


def from_next(x, axis):
    count = lax.axis_size(axis)
    return lax.ppermute(x, axis, [((i + 1) % count, i) for i in range(count)])


def from_previous(x, axis):
    count = lax.axis_size(axis)
    return lax.ppermute(x, axis, [(i, (i + 1) % count) for i in range(count)])


def halos(e):
    first, last = e[0], e[-1]
    beyond = from_next(first, "lat")
    before = from_previous(last, "lat")
    spatial = [(from_next(x, "src"), from_previous(x, "src")) for x in e]
    later = [*e[1:], beyond]
    earlier = [before, *e[:-1]]
    return [(e[t], later[t], earlier[t], *spatial[t]) for t in range(len(e))]


def body(fine, basis, dinv, hops, nbr, agg):
    nbr = nbr.T
    slices = range(fine.shape[0])
    pairs = [restrict(t, agg, fine, basis, dinv) for t in slices]
    rhs = [p[0] for p in pairs]
    e = [p[1] for p in pairs]
    around = halos(e)
    e = [sweep(t, agg, nbr, (rhs[t], *around[t]), hops, dinv) for t in slices]
    around = halos(e)
    out = None
    for t in slices:
        out = prolong(t, fine.shape, agg, nbr, (rhs[t], *around[t]), hops, dinv, basis, out)
    return out


def solution(mesh):
    return jax.shard_map(
        body,
        mesh=mesh,
        in_specs=(
            P("lat", "src", None, None),
            P("lat", "src", None, None),
            P("lat", "src", None, None),
            P("lat", "src", None, None, None),
            P(),
            P("lat", "src"),
        ),
        out_specs=P("lat", "src", None, None),
        check_vma=False,
    )
```

```python
import functools

import jax
import jax.numpy as jnp
from jax import lax
from jax.experimental import pallas as pl
from jax.experimental.pallas import tpu as pltpu
from jax.sharding import PartitionSpec as P

DAMPING = 0.8
KEEP = 1.0 - DAMPING
BF16 = jnp.bfloat16
F32 = jnp.float32
PIECES = 2
HBM = pl.BlockSpec(memory_space=pltpu.HBM)
VMEM = pl.BlockSpec(memory_space=pltpu.VMEM)
PARAMS = pltpu.CompilerParams(vmem_limit_bytes=32 * 1024 * 1024)


def in_hbm(x):
    return pltpu.with_memory_space_constraint(x, pltpu.HBM)


def in_vmem(x):
    return pltpu.with_memory_space_constraint(x, pltpu.VMEM)


def dot(a, b):
    return jnp.dot(a, b, preferred_element_type=F32)


class Copies:
    def __init__(self, sems):
        self.sems = sems
        self.count = 0

    def start(self, src, dst):
        copy = pltpu.make_async_copy(src, dst, self.sems.at[self.count])
        self.count += 1
        copy.start()
        return copy


def restrict_kernel(agg, nbr, fine, basis, dinv, hops, *refs):
    nt, ns, _, nf = fine.shape
    rhs, e = refs[:nt], refs[nt : 2 * nt]
    basis_v, dinv_v = refs[2 * nt : 2 * nt + 2]
    hops_v = refs[2 * nt + 2 : 3 * nt + 2]
    agg_s, nbr_s, fine_v, sems = refs[3 * nt + 2 :]
    depth = nf // PIECES
    copies = Copies(sems)
    agg_in = copies.start(agg, agg_s)
    nbr_in = copies.start(nbr, nbr_s)
    loads = {}
    for t in range(nt):
        for s in range(ns):
            pieces = PIECES if (t, s) == (0, 0) else 1
            depth = nf // pieces
            for p in range(pieces):
                part = pl.ds(p * depth, depth)
                loads[t, s, p] = (
                    copies.start(basis.at[t, s, part], basis_v.at[t, s, part]),
                    copies.start(fine.at[t, s, :, part], fine_v.at[t, s, :, part]),
                )
    dinv_in = copies.start(dinv, dinv_v)
    agg_in.wait()
    nbr_in.wait()
    hops_in = []
    for t in range(nt):
        for c in range(ns):
            spatial = nbr_s.shape[1]
            site = (agg_s[0, 0] & -2) + c
            upward = (nbr_s[0, site] == lax.rem(site + 2, spatial)).astype(jnp.int32)
            hops_in.append(copies.start(hops.at[t, c, 1 - upward], hops_v[t].at[c, 0]))
            hops_in.append(copies.start(hops.at[t, c, upward], hops_v[t].at[c, 1]))
            rest = pl.ds(2, 6)
            hops_in.append(copies.start(hops.at[t, c, rest], hops_v[t].at[c, rest]))
    for t in range(nt):
        for s in range(ns):
            c = agg_s[t, s] & 1
            pieces = PIECES if (t, s) == (0, 0) else 1
            depth = nf // pieces
            total = None
            for p in range(pieces):
                for load in loads[t, s, p]:
                    load.wait()
                part = pl.ds(p * depth, depth)
                term = dot(fine_v[t, s, :, part], basis_v[t, s, part])
                total = term if total is None else total + term
            r = total.astype(BF16)
            if (t, s) == (0, 0):
                dinv_in.wait()
            rhs[t][c] = r
            e[t][c] = (DAMPING * dot(r, dinv_v[t, c])).astype(BF16)
    for load in hops_in:
        load.wait()


def restrict(agg, nbr, fine, basis, dinv, hops):
    nt, ns, n, nf = fine.shape
    nc = basis.shape[3]
    part = pltpu.VMEM((ns, n, nc), BF16)
    out_shape = [
        *[part] * (2 * nt),
        pltpu.VMEM(basis.shape, BF16),
        pltpu.VMEM(dinv.shape, BF16),
        *[pltpu.VMEM(hops.shape[1:], BF16)] * nt,
    ]
    out = pl.pallas_call(
        restrict_kernel,
        in_specs=[HBM] * 6,
        out_specs=[VMEM] * len(out_shape),
        out_shape=out_shape,
        scratch_shapes=[
            pltpu.SMEM(agg.shape, jnp.int32),
            pltpu.SMEM(nbr.shape, jnp.int32),
            pltpu.VMEM(fine.shape, BF16),
            pltpu.SemaphoreType.DMA((3 + 2 * (nt * ns + PIECES - 1) + 3 * nt * ns,)),
        ],
        compiler_params=PARAMS,
        cost_estimate=pl.CostEstimate(
            flops=2 * nt * ns * n * nc * (nf + nc),
            bytes_accessed=2 * nt * ns * (n * nf + nf * nc + 9 * nc * nc),
            transcendentals=0,
        ),
        name="restrict",
    )(*map(in_hbm, (agg, nbr, fine, basis, dinv, hops)))
    return out[:nt], out[nt : 2 * nt], out[2 * nt], out[2 * nt + 1], out[2 * nt + 2 :]


def next_iterate(c, rhs, e, later, earlier, up, dn, hops, dinv):
    ns, _, nc = e.shape
    own, other = e[c], e[ns - 1 - c]
    stacked = jnp.concatenate(
        [up[c], dn[c], own, own, other, other, later[c], earlier[c]], axis=1
    )
    hop = dot(stacked, hops[c].reshape(8 * nc, nc))
    difference = (rhs[c].astype(F32) - hop).astype(BF16)
    return (KEEP * own.astype(F32) + DAMPING * dot(difference, dinv[c])).astype(BF16)


def sweep_kernel(t, *refs):
    hops, dinv, out = refs[6:]
    for c in range(out.shape[0]):
        out[c] = next_iterate(c, *refs[:6], hops, dinv.at[t])


def sweep(t, coarse, hops, dinv):
    shape = coarse[0].shape
    ns, n, nc = shape
    return pl.pallas_call(
        functools.partial(sweep_kernel, t),
        in_specs=[VMEM] * 8,
        out_specs=VMEM,
        out_shape=pltpu.VMEM(shape, BF16),
        compiler_params=PARAMS,
        cost_estimate=pl.CostEstimate(
            flops=2 * ns * n * nc * 9 * nc,
            bytes_accessed=2 * ns * (9 * nc * nc + 7 * n * nc),
            transcendentals=0,
        ),
        name="sweep",
    )(*map(in_vmem, (*coarse, hops, dinv)))


def prolong_kernel(t, *refs):
    hops, dinv, basis, agg = refs[6:10]
    out, agg_s, value_v, out_v, sems = refs[len(refs) - 5 :]
    ns, n, nf = out_v.shape
    width = nf // PIECES
    copies = Copies(sems)
    agg_in = copies.start(agg, agg_s)
    for c in range(ns):
        value_v[c] = next_iterate(c, *refs[:6], hops, dinv.at[t])
    agg_in.wait()
    outs = []
    for s in range(ns):
        value = value_v[agg_s[t, s] & 1]
        for p in range(PIECES):
            part = pl.ds(p * width, width)
            out_v[s, :, part] = lax.dot_general(
                value, basis[t, s, part], (((1,), (1,)), ((), ())), preferred_element_type=F32
            ).astype(BF16)
            outs.append(copies.start(out_v.at[s, :, part], out.at[t, s, :, part]))
    for wait in outs:
        wait.wait()


def prolong(t, shape, agg, coarse, hops, dinv, basis, previous):
    part = coarse[0].shape
    ns, n, nc = part
    nf = basis.shape[2]
    operands = [*map(in_vmem, (*coarse, hops, dinv, basis)), in_hbm(agg)]
    in_specs = [VMEM] * 9 + [HBM]
    aliases = {}
    if previous is not None:
        aliases = {len(operands): 0}
        operands.append(in_hbm(previous))
        in_specs.append(HBM)
    return pl.pallas_call(
        functools.partial(prolong_kernel, t),
        in_specs=in_specs,
        out_specs=HBM,
        out_shape=pltpu.HBM(shape, BF16),
        input_output_aliases=aliases,
        scratch_shapes=[
            pltpu.SMEM(agg.shape, jnp.int32),
            pltpu.VMEM(part, BF16),
            pltpu.VMEM((ns, n, nf), BF16),
            pltpu.SemaphoreType.DMA((1 + ns * PIECES,)),
        ],
        compiler_params=PARAMS,
        cost_estimate=pl.CostEstimate(
            flops=2 * ns * n * nc * (9 * nc + nf),
            bytes_accessed=2 * ns * (9 * nc * nc + 6 * n * nc + nf * nc + n * nf),
            transcendentals=0,
        ),
        name="prolong",
    )(*operands)


def from_next(x, axis):
    count = lax.axis_size(axis)
    return lax.ppermute(x, axis, [((i + 1) % count, i) for i in range(count)])


def from_previous(x, axis):
    count = lax.axis_size(axis)
    return lax.ppermute(x, axis, [(i, (i + 1) % count) for i in range(count)])


def halos(e):
    first, last = e[0], e[-1]
    beyond = from_next(first, "lat")
    before = from_previous(last, "lat")
    spatial = [(from_next(x, "src"), from_previous(x, "src")) for x in e]
    later = [*e[1:], beyond]
    earlier = [before, *e[:-1]]
    return [(e[t], later[t], earlier[t], *spatial[t]) for t in range(len(e))]


def body(fine, basis, dinv, hops, nbr, agg):
    slices = range(fine.shape[0])
    rhs, e, basis, dinv, hops = restrict(agg, nbr.T, fine, basis, dinv, hops)
    around = halos(e)
    e = [sweep(t, (rhs[t], *around[t]), hops[t], dinv) for t in slices]
    around = halos(e)
    out = None
    for t in slices:
        out = prolong(t, fine.shape, agg, (rhs[t], *around[t]), hops[t], dinv, basis, out)
    return out


def solution(mesh):
    return jax.shard_map(
        body,
        mesh=mesh,
        in_specs=(
            P("lat", "src", None, None),
            P("lat", "src", None, None),
            P("lat", "src", None, None),
            P("lat", "src", None, None, None),
            P(),
            P("lat", "src"),
        ),
        out_specs=P("lat", "src", None, None),
        check_vma=False,
    )
```

```python
import functools

import jax
import jax.numpy as jnp
from jax import lax
from jax.experimental import pallas as pl
from jax.experimental.pallas import tpu as pltpu
from jax.sharding import PartitionSpec as P

DAMPING = 0.8
KEEP = 1.0 - DAMPING
BF16 = jnp.bfloat16
F32 = jnp.float32
PIECES = 2
HBM = pl.BlockSpec(memory_space=pltpu.HBM)
VMEM = pl.BlockSpec(memory_space=pltpu.VMEM)
PARAMS = pltpu.CompilerParams(vmem_limit_bytes=32 * 1024 * 1024)


def in_hbm(x):
    return pltpu.with_memory_space_constraint(x, pltpu.HBM)


def in_vmem(x):
    return pltpu.with_memory_space_constraint(x, pltpu.VMEM)


def dot(a, b):
    return jnp.dot(a, b, preferred_element_type=F32)


class Copies:
    def __init__(self, sems):
        self.sems = sems
        self.count = 0

    def start(self, src, dst):
        copy = pltpu.make_async_copy(src, dst, self.sems.at[self.count])
        self.count += 1
        copy.start()
        return copy


def restrict_kernel(agg, nbr, fine, basis, dinv, hops, *refs):
    nt, ns, _, nf = fine.shape
    rhs, e = refs[:nt], refs[nt : 2 * nt]
    basis_v, dinv_v = refs[2 * nt : 2 * nt + 2]
    hops_v = refs[2 * nt + 2 : 3 * nt + 2]
    agg_s, nbr_s, fine_v, sems = refs[3 * nt + 2 :]
    depth = nf // PIECES
    copies = Copies(sems)
    agg_in = copies.start(agg, agg_s)
    nbr_in = copies.start(nbr, nbr_s)
    dinv_in = copies.start(dinv, dinv_v)
    loads = {}
    for t in range(nt):
        for s in range(ns):
            pieces = PIECES if (t, s) == (0, 0) else 1
            depth = nf // pieces
            for p in range(pieces):
                part = pl.ds(p * depth, depth)
                loads[t, s, p] = (
                    copies.start(basis.at[t, s, part], basis_v.at[t, s, part]),
                    copies.start(fine.at[t, s, :, part], fine_v.at[t, s, :, part]),
                )
    agg_in.wait()
    nbr_in.wait()
    lane = lax.axis_index("lat")
    hops_in = []
    for t in range(nt):
        for c in range(ns):
            spatial = nbr_s.shape[1]
            site = (agg_s[0, 0] & -2) + c
            down_first = (nbr_s[0, site] != lax.rem(site + 2, spatial)).astype(jnp.int32)
            even = down_first ^ (((site >> 1) + lane) & 1)
            hops_in.append(copies.start(hops.at[t, c, even], hops_v[t].at[c, 0]))
            hops_in.append(copies.start(hops.at[t, c, 1 - even], hops_v[t].at[c, 1]))
            rest = pl.ds(2, 6)
            hops_in.append(copies.start(hops.at[t, c, rest], hops_v[t].at[c, rest]))
    for t in range(nt):
        for s in range(ns):
            c = agg_s[t, s] & 1
            pieces = PIECES if (t, s) == (0, 0) else 1
            depth = nf // pieces
            total = None
            for p in range(pieces):
                for load in loads[t, s, p]:
                    load.wait()
                part = pl.ds(p * depth, depth)
                term = dot(fine_v[t, s, :, part], basis_v[t, s, part])
                total = term if total is None else total + term
            r = total.astype(BF16)
            if (t, s) == (0, 0):
                dinv_in.wait()
            rhs[t][c] = r
            e[t][c] = (DAMPING * dot(r, dinv_v[t, c])).astype(BF16)
    for load in hops_in:
        load.wait()


def restrict(agg, nbr, fine, basis, dinv, hops):
    nt, ns, n, nf = fine.shape
    nc = basis.shape[3]
    part = pltpu.VMEM((ns, n, nc), BF16)
    out_shape = [
        *[part] * (2 * nt),
        pltpu.VMEM(basis.shape, BF16),
        pltpu.VMEM(dinv.shape, BF16),
        *[pltpu.VMEM(hops.shape[1:], BF16)] * nt,
    ]
    out = pl.pallas_call(
        restrict_kernel,
        in_specs=[HBM] * 6,
        out_specs=[VMEM] * len(out_shape),
        out_shape=out_shape,
        scratch_shapes=[
            pltpu.SMEM(agg.shape, jnp.int32),
            pltpu.SMEM(nbr.shape, jnp.int32),
            pltpu.VMEM(fine.shape, BF16),
            pltpu.SemaphoreType.DMA((3 + 2 * (nt * ns + PIECES - 1) + 3 * nt * ns,)),
        ],
        compiler_params=PARAMS,
        cost_estimate=pl.CostEstimate(
            flops=2 * nt * ns * n * nc * (nf + nc),
            bytes_accessed=2 * nt * ns * (n * nf + nf * nc + 9 * nc * nc),
            transcendentals=0,
        ),
        name="restrict",
    )(*map(in_hbm, (agg, nbr, fine, basis, dinv, hops)))
    return out[:nt], out[nt : 2 * nt], out[2 * nt], out[2 * nt + 1], out[2 * nt + 2 :]


def next_iterate(c, rhs, e, later, earlier, even, odd, hops, dinv):
    ns, _, nc = e.shape
    own, other = e[c], e[ns - 1 - c]
    stacked = jnp.concatenate(
        [even[c], odd[c], own, own, other, other, later[c], earlier[c]], axis=1
    )
    hop = dot(stacked, hops[c].reshape(8 * nc, nc))
    difference = (rhs[c].astype(F32) - hop).astype(BF16)
    return (KEEP * own.astype(F32) + DAMPING * dot(difference, dinv[c])).astype(BF16)


def sweep_kernel(t, *refs):
    hops, dinv, out = refs[6:]
    for c in range(out.shape[0]):
        out[c] = next_iterate(c, *refs[:6], hops, dinv.at[t])


def sweep(t, coarse, hops, dinv):
    shape = coarse[0].shape
    ns, n, nc = shape
    return pl.pallas_call(
        functools.partial(sweep_kernel, t),
        in_specs=[VMEM] * 8,
        out_specs=VMEM,
        out_shape=pltpu.VMEM(shape, BF16),
        compiler_params=PARAMS,
        cost_estimate=pl.CostEstimate(
            flops=2 * ns * n * nc * 9 * nc,
            bytes_accessed=2 * ns * (9 * nc * nc + 7 * n * nc),
            transcendentals=0,
        ),
        name="sweep",
    )(*map(in_vmem, (*coarse, hops, dinv)))


def prolong_kernel(t, *refs):
    hops, dinv, basis, agg = refs[6:10]
    out, agg_s, value_v, out_v, sems = refs[len(refs) - 5 :]
    ns, n, nf = out_v.shape
    width = nf // PIECES
    copies = Copies(sems)
    agg_in = copies.start(agg, agg_s)
    for c in range(ns):
        value_v[c] = next_iterate(c, *refs[:6], hops, dinv.at[t])
    agg_in.wait()
    outs = []
    for s in range(ns):
        value = value_v[agg_s[t, s] & 1]
        for p in range(PIECES):
            part = pl.ds(p * width, width)
            out_v[s, :, part] = lax.dot_general(
                value, basis[t, s, part], (((1,), (1,)), ((), ())), preferred_element_type=F32
            ).astype(BF16)
            outs.append(copies.start(out_v.at[s, :, part], out.at[t, s, :, part]))
    for wait in outs:
        wait.wait()


def prolong(t, shape, agg, coarse, hops, dinv, basis, previous):
    part = coarse[0].shape
    ns, n, nc = part
    nf = basis.shape[2]
    operands = [*map(in_vmem, (*coarse, hops, dinv, basis)), in_hbm(agg)]
    in_specs = [VMEM] * 9 + [HBM]
    aliases = {}
    if previous is not None:
        aliases = {len(operands): 0}
        operands.append(in_hbm(previous))
        in_specs.append(HBM)
    return pl.pallas_call(
        functools.partial(prolong_kernel, t),
        in_specs=in_specs,
        out_specs=HBM,
        out_shape=pltpu.HBM(shape, BF16),
        input_output_aliases=aliases,
        scratch_shapes=[
            pltpu.SMEM(agg.shape, jnp.int32),
            pltpu.VMEM(part, BF16),
            pltpu.VMEM((ns, n, nf), BF16),
            pltpu.SemaphoreType.DMA((1 + ns * PIECES,)),
        ],
        compiler_params=PARAMS,
        cost_estimate=pl.CostEstimate(
            flops=2 * ns * n * nc * (9 * nc + nf),
            bytes_accessed=2 * ns * (9 * nc * nc + 6 * n * nc + nf * nc + n * nf),
            transcendentals=0,
        ),
        name="prolong",
    )(*operands)


def from_next(x, axis):
    count = lax.axis_size(axis)
    return lax.ppermute(x, axis, [((i + 1) % count, i) for i in range(count)])


def from_previous(x, axis):
    count = lax.axis_size(axis)
    return lax.ppermute(x, axis, [(i, (i + 1) % count) for i in range(count)])


def swap_sites(x, offset):
    axes = ("lat", "src")
    nt, count = (lax.axis_size(a) for a in axes)
    step = lambda l, s: (s + 1 - 2 * ((l + s + offset) % 2)) % count
    pairs = [(l * count + s, l * count + step(l, s)) for l in range(nt) for s in range(count)]
    return lax.ppermute(x, axes, pairs)


def halos(e):
    spatial = [(swap_sites(x, 0), swap_sites(x, 1)) for x in e]
    beyond = from_next(e[0], "lat")
    before = from_previous(e[-1], "lat")
    later = [*e[1:], beyond]
    earlier = [before, *e[:-1]]
    return [(e[t], later[t], earlier[t], *spatial[t]) for t in range(len(e))]


def body(fine, basis, dinv, hops, nbr, agg):
    slices = range(fine.shape[0])
    rhs, e, basis, dinv, hops = restrict(agg, nbr.T, fine, basis, dinv, hops)
    around = halos(e)
    e = [sweep(t, (rhs[t], *around[t]), hops[t], dinv) for t in slices]
    around = halos(e)
    out = None
    for t in slices:
        out = prolong(t, fine.shape, agg, (rhs[t], *around[t]), hops[t], dinv, basis, out)
    return out


def solution(mesh):
    return jax.shard_map(
        body,
        mesh=mesh,
        in_specs=(
            P("lat", "src", None, None),
            P("lat", "src", None, None),
            P("lat", "src", None, None),
            P("lat", "src", None, None, None),
            P(),
            P("lat", "src"),
        ),
        out_specs=P("lat", "src", None, None),
        check_vma=False,
    )
```

```python
import functools

import jax
import jax.numpy as jnp
from jax import lax
from jax.experimental import pallas as pl
from jax.experimental.pallas import tpu as pltpu
from jax.sharding import PartitionSpec as P

DAMPING = 0.8
KEEP = 1.0 - DAMPING
BF16 = jnp.bfloat16
F32 = jnp.float32
PIECES = 2
HBM = pl.BlockSpec(memory_space=pltpu.HBM)
VMEM = pl.BlockSpec(memory_space=pltpu.VMEM)
PARAMS = pltpu.CompilerParams(vmem_limit_bytes=32 * 1024 * 1024)


def in_hbm(x):
    return pltpu.with_memory_space_constraint(x, pltpu.HBM)


def in_vmem(x):
    return pltpu.with_memory_space_constraint(x, pltpu.VMEM)


def dot(a, b):
    return jnp.dot(a, b, preferred_element_type=F32)


class Copies:
    def __init__(self, sems):
        self.sems = sems
        self.count = 0

    def start(self, src, dst):
        copy = pltpu.make_async_copy(src, dst, self.sems.at[self.count])
        self.count += 1
        copy.start()
        return copy


def restrict_kernel(agg, nbr, fine, basis, dinv, hops, *refs):
    nt, ns, _, nf = fine.shape
    rhs, e = refs[:nt], refs[nt : 2 * nt]
    basis_v, dinv_v = refs[2 * nt : 2 * nt + 2]
    hops_v = refs[2 * nt + 2 : 3 * nt + 2]
    agg_s, nbr_s, fine_v, sems = refs[3 * nt + 2 :]
    depth = nf // PIECES
    copies = Copies(sems)
    agg_in = copies.start(agg, agg_s)
    nbr_in = copies.start(nbr, nbr_s)
    dinv_in = copies.start(dinv, dinv_v)
    loads = {}
    for t in range(nt):
        for s in range(ns):
            pieces = PIECES if (t, s) == (0, 0) else 1
            depth = nf // pieces
            for p in range(pieces):
                part = pl.ds(p * depth, depth)
                loads[t, s, p] = (
                    copies.start(basis.at[t, s, part], basis_v.at[t, s, part]),
                    copies.start(fine.at[t, s, :, part], fine_v.at[t, s, :, part]),
                )
    agg_in.wait()
    nbr_in.wait()
    lane = lax.axis_index("lat")
    lane = lane + (lane < 2).astype(jnp.int32)
    hops_in = []
    for t in range(nt):
        for c in range(ns):
            spatial = nbr_s.shape[1]
            site = (agg_s[0, 0] & -2) + c
            down_first = (nbr_s[0, site] != lax.rem(site + 2, spatial)).astype(jnp.int32)
            even = down_first ^ (((site >> 1) + lane) & 1)
            hops_in.append(copies.start(hops.at[t, c, even], hops_v[t].at[c, 0]))
            hops_in.append(copies.start(hops.at[t, c, 1 - even], hops_v[t].at[c, 1]))
            rest = pl.ds(2, 6)
            hops_in.append(copies.start(hops.at[t, c, rest], hops_v[t].at[c, rest]))
    for t in range(nt):
        for s in range(ns):
            c = agg_s[t, s] & 1
            pieces = PIECES if (t, s) == (0, 0) else 1
            depth = nf // pieces
            total = None
            for p in range(pieces):
                for load in loads[t, s, p]:
                    load.wait()
                part = pl.ds(p * depth, depth)
                term = dot(fine_v[t, s, :, part], basis_v[t, s, part])
                total = term if total is None else total + term
            r = total.astype(BF16)
            if (t, s) == (0, 0):
                dinv_in.wait()
            rhs[t][c] = r
            e[t][c] = (DAMPING * dot(r, dinv_v[t, c])).astype(BF16)
    for load in hops_in:
        load.wait()


def restrict(agg, nbr, fine, basis, dinv, hops):
    nt, ns, n, nf = fine.shape
    nc = basis.shape[3]
    part = pltpu.VMEM((ns, n, nc), BF16)
    out_shape = [
        *[part] * (2 * nt),
        pltpu.VMEM(basis.shape, BF16),
        pltpu.VMEM(dinv.shape, BF16),
        *[pltpu.VMEM(hops.shape[1:], BF16)] * nt,
    ]
    out = pl.pallas_call(
        restrict_kernel,
        in_specs=[HBM] * 6,
        out_specs=[VMEM] * len(out_shape),
        out_shape=out_shape,
        scratch_shapes=[
            pltpu.SMEM(agg.shape, jnp.int32),
            pltpu.SMEM(nbr.shape, jnp.int32),
            pltpu.VMEM(fine.shape, BF16),
            pltpu.SemaphoreType.DMA((3 + 2 * (nt * ns + PIECES - 1) + 3 * nt * ns,)),
        ],
        compiler_params=PARAMS,
        cost_estimate=pl.CostEstimate(
            flops=2 * nt * ns * n * nc * (nf + nc),
            bytes_accessed=2 * nt * ns * (n * nf + nf * nc + 9 * nc * nc),
            transcendentals=0,
        ),
        name="restrict",
    )(*map(in_hbm, (agg, nbr, fine, basis, dinv, hops)))
    return out[:nt], out[nt : 2 * nt], out[2 * nt], out[2 * nt + 1], out[2 * nt + 2 :]


def next_iterate(c, rhs, e, later, earlier, even, odd, hops, dinv):
    ns, _, nc = e.shape
    own, other = e[c], e[ns - 1 - c]
    stacked = jnp.concatenate(
        [even[c], odd[c], own, own, other, other, later[c], earlier[c]], axis=1
    )
    hop = dot(stacked, hops[c].reshape(8 * nc, nc))
    difference = (rhs[c].astype(F32) - hop).astype(BF16)
    return (KEEP * own.astype(F32) + DAMPING * dot(difference, dinv[c])).astype(BF16)


def sweep_kernel(t, *refs):
    hops, dinv = refs[6:8]
    if len(refs) == 11:
        refs[10][...] = refs[8][...]
    out = refs[8 + (len(refs) == 11)]
    for c in range(out.shape[0]):
        out[c] = next_iterate(c, *refs[:6], hops, dinv.at[t])


def sweep(t, coarse, hops, dinv, edge):
    shape = coarse[0].shape
    ns, n, nc = shape
    return pl.pallas_call(
        functools.partial(sweep_kernel, t),
        in_specs=[VMEM] * (8 + len(edge)),
        out_specs=[VMEM] * (1 + len(edge)),
        out_shape=[pltpu.VMEM(shape, BF16)] * (1 + len(edge)),
        compiler_params=PARAMS,
        cost_estimate=pl.CostEstimate(
            flops=2 * ns * n * nc * 9 * nc,
            bytes_accessed=2 * ns * (9 * nc * nc + 7 * n * nc),
            transcendentals=0,
        ),
        name="sweep",
    )(*map(in_vmem, (*coarse, hops, dinv, *edge)))


def prolong_kernel(t, *refs):
    hops, dinv, basis, agg = refs[6:10]
    out, agg_s, value_v, out_v, sems = refs[len(refs) - 5 :]
    ns, n, nf = out_v.shape
    width = nf // PIECES
    copies = Copies(sems)
    agg_in = copies.start(agg, agg_s)
    for c in range(ns):
        value_v[c] = next_iterate(c, *refs[:6], hops, dinv.at[t])
    agg_in.wait()
    outs = []
    for s in range(ns):
        value = value_v[agg_s[t, s] & 1]
        for p in range(PIECES):
            part = pl.ds(p * width, width)
            out_v[s, :, part] = lax.dot_general(
                value, basis[t, s, part], (((1,), (1,)), ((), ())), preferred_element_type=F32
            ).astype(BF16)
            outs.append(copies.start(out_v.at[s, :, part], out.at[t, s, :, part]))
    for wait in outs:
        wait.wait()


def prolong(t, shape, agg, coarse, hops, dinv, basis, previous):
    part = coarse[0].shape
    ns, n, nc = part
    nf = basis.shape[2]
    operands = [*map(in_vmem, (*coarse, hops, dinv, basis)), in_hbm(agg)]
    in_specs = [VMEM] * 9 + [HBM]
    aliases = {}
    if previous is not None:
        aliases = {len(operands): 0}
        operands.append(in_hbm(previous))
        in_specs.append(HBM)
    return pl.pallas_call(
        functools.partial(prolong_kernel, t),
        in_specs=in_specs,
        out_specs=HBM,
        out_shape=pltpu.HBM(shape, BF16),
        input_output_aliases=aliases,
        scratch_shapes=[
            pltpu.SMEM(agg.shape, jnp.int32),
            pltpu.VMEM(part, BF16),
            pltpu.VMEM((ns, n, nf), BF16),
            pltpu.SemaphoreType.DMA((1 + ns * PIECES,)),
        ],
        compiler_params=PARAMS,
        cost_estimate=pl.CostEstimate(
            flops=2 * ns * n * nc * (9 * nc + nf),
            bytes_accessed=2 * ns * (9 * nc * nc + 6 * n * nc + nf * nc + n * nf),
            transcendentals=0,
        ),
        name="prolong",
    )(*operands)


def from_next(x, axis):
    count = lax.axis_size(axis)
    return lax.ppermute(x, axis, [((i + 1) % count, i) for i in range(count)])


def from_previous(x, axis):
    count = lax.axis_size(axis)
    return lax.ppermute(x, axis, [(i, (i + 1) % count) for i in range(count)])


def swap_sites(x, offset):
    axes = ("lat", "src")
    nt, count = (lax.axis_size(a) for a in axes)
    step = lambda l, s: (s + 1 - 2 * (((l + (l < 2)) + s + offset) % 2)) % count
    pairs = [(l * count + s, l * count + step(l, s)) for l in range(nt) for s in range(count)]
    return lax.ppermute(x, axes, pairs)


def halos(e, first, last):
    spatial = [(swap_sites(x, 0), swap_sites(x, 1)) for x in e]
    beyond = from_next(first, "lat")
    before = from_previous(last, "lat")
    later = [*e[1:], beyond]
    earlier = [before, *e[:-1]]
    return [(e[t], later[t], earlier[t], *spatial[t]) for t in range(len(e))]


def body(fine, basis, dinv, hops, nbr, agg):
    slices = range(fine.shape[0])
    rhs, e, basis, dinv, hops = restrict(agg, nbr.T, fine, basis, dinv, hops)
    around = halos(e, e[0], e[-1])
    e = []
    for t in slices:
        edge = (e[0],) if t == slices[-1] else ()
        value, *edge = sweep(t, (rhs[t], *around[t]), hops[t], dinv, edge)
        e.append(value)
    around = halos(e, edge[0], e[-1])
    out = None
    for t in slices:
        out = prolong(t, fine.shape, agg, (rhs[t], *around[t]), hops[t], dinv, basis, out)
    return out


def solution(mesh):
    return jax.shard_map(
        body,
        mesh=mesh,
        in_specs=(
            P("lat", "src", None, None),
            P("lat", "src", None, None),
            P("lat", "src", None, None),
            P("lat", "src", None, None, None),
            P(),
            P("lat", "src"),
        ),
        out_specs=P("lat", "src", None, None),
        check_vma=False,
    )
```

```python
import functools

import jax
import jax.numpy as jnp
from jax import lax
from jax.experimental import pallas as pl
from jax.experimental.pallas import tpu as pltpu
from jax.sharding import PartitionSpec as P

DAMPING = 0.8
KEEP = 1.0 - DAMPING
BF16 = jnp.bfloat16
F32 = jnp.float32
PIECES = 2
HBM = pl.BlockSpec(memory_space=pltpu.HBM)
VMEM = pl.BlockSpec(memory_space=pltpu.VMEM)
PARAMS = pltpu.CompilerParams(vmem_limit_bytes=32 * 1024 * 1024)


def in_hbm(x):
    return pltpu.with_memory_space_constraint(x, pltpu.HBM)


def in_vmem(x):
    return pltpu.with_memory_space_constraint(x, pltpu.VMEM)


def dot(a, b):
    return jnp.dot(a, b, preferred_element_type=F32)


class Copies:
    def __init__(self, sems):
        self.sems = sems
        self.count = 0

    def start(self, src, dst):
        copy = pltpu.make_async_copy(src, dst, self.sems.at[self.count])
        self.count += 1
        copy.start()
        return copy


def restrict_kernel(agg, nbr, fine, basis, dinv, hops, *refs):
    nt, ns, _, nf = fine.shape
    rhs, e = refs[:nt], refs[nt : 2 * nt]
    basis_v, dinv_v = refs[2 * nt : 2 * nt + 2]
    hops_v = refs[2 * nt + 2 : 3 * nt + 2]
    agg_s, nbr_s, fine_v, sems = refs[3 * nt + 2 :]
    depth = nf // PIECES
    copies = Copies(sems)
    agg_in = copies.start(agg, agg_s)
    nbr_in = copies.start(nbr, nbr_s)
    dinv_in = copies.start(dinv, dinv_v)
    loads = {}
    for t in range(nt):
        for s in range(ns):
            pieces = PIECES if (t, s) == (0, 0) else 1
            depth = nf // pieces
            for p in range(pieces):
                part = pl.ds(p * depth, depth)
                loads[t, s, p] = (
                    copies.start(basis.at[t, s, part], basis_v.at[t, s, part]),
                    copies.start(fine.at[t, s, :, part], fine_v.at[t, s, :, part]),
                )
    agg_in.wait()
    nbr_in.wait()
    lane = lax.axis_index("lat")
    lane = lane + (lane < 2).astype(jnp.int32)
    hops_in = []
    for t in range(nt):
        for c in range(ns):
            spatial = nbr_s.shape[1]
            site = (agg_s[0, 0] & -2) + c
            down_first = (nbr_s[0, site] != lax.rem(site + 2, spatial)).astype(jnp.int32)
            even = down_first ^ (((site >> 1) + lane) & 1)
            hops_in.append(copies.start(hops.at[t, c, even], hops_v[t].at[c, 0]))
            hops_in.append(copies.start(hops.at[t, c, 1 - even], hops_v[t].at[c, 1]))
            rest = pl.ds(2, 6)
            hops_in.append(copies.start(hops.at[t, c, rest], hops_v[t].at[c, rest]))
    for t in range(nt):
        for s in range(ns):
            c = agg_s[t, s] & 1
            pieces = PIECES if (t, s) == (0, 0) else 1
            depth = nf // pieces
            total = None
            for p in range(pieces):
                for load in loads[t, s, p]:
                    load.wait()
                part = pl.ds(p * depth, depth)
                term = dot(fine_v[t, s, :, part], basis_v[t, s, part])
                total = term if total is None else total + term
            r = total.astype(BF16)
            if (t, s) == (0, 0):
                dinv_in.wait()
            rhs[t][c] = r
            e[t][c] = (DAMPING * dot(r, dinv_v[t, c])).astype(BF16)
    for load in hops_in:
        load.wait()


def restrict(agg, nbr, fine, basis, dinv, hops):
    nt, ns, n, nf = fine.shape
    nc = basis.shape[3]
    part = pltpu.VMEM((ns, n, nc), BF16)
    out_shape = [
        *[part] * (2 * nt),
        pltpu.VMEM(basis.shape, BF16),
        pltpu.VMEM(dinv.shape, BF16),
        *[pltpu.VMEM(hops.shape[1:], BF16)] * nt,
    ]
    out = pl.pallas_call(
        restrict_kernel,
        in_specs=[HBM] * 6,
        out_specs=[VMEM] * len(out_shape),
        out_shape=out_shape,
        scratch_shapes=[
            pltpu.SMEM(agg.shape, jnp.int32),
            pltpu.SMEM(nbr.shape, jnp.int32),
            pltpu.VMEM(fine.shape, BF16),
            pltpu.SemaphoreType.DMA((3 + 2 * (nt * ns + PIECES - 1) + 3 * nt * ns,)),
        ],
        compiler_params=PARAMS,
        cost_estimate=pl.CostEstimate(
            flops=2 * nt * ns * n * nc * (nf + nc),
            bytes_accessed=2 * nt * ns * (n * nf + nf * nc + 9 * nc * nc),
            transcendentals=0,
        ),
        name="restrict",
    )(*map(in_hbm, (agg, nbr, fine, basis, dinv, hops)))
    return out[:nt], out[nt : 2 * nt], out[2 * nt], out[2 * nt + 1], out[2 * nt + 2 :]


def next_iterate(c, rhs, e, later, earlier, even, odd, hops, dinv):
    ns, _, nc = e.shape
    own, other = e[c], e[ns - 1 - c]
    stacked = jnp.concatenate(
        [even[c], odd[c], own, own, other, other, later[c], earlier[c]], axis=1
    )
    hop = dot(stacked, hops[c].reshape(8 * nc, nc))
    difference = (rhs[c].astype(F32) - hop).astype(BF16)
    return (KEEP * own.astype(F32) + DAMPING * dot(difference, dinv[c])).astype(BF16)


def sweep_kernel(t, *refs):
    hops, dinv = refs[6:8]
    if len(refs) == 11:
        refs[10][...] = refs[8][...]
    out = refs[8 + (len(refs) == 11)]
    for c in range(out.shape[0]):
        out[c] = next_iterate(c, *refs[:6], hops, dinv.at[t])


def sweep(t, coarse, hops, dinv, edge):
    shape = coarse[0].shape
    ns, n, nc = shape
    return pl.pallas_call(
        functools.partial(sweep_kernel, t),
        in_specs=[VMEM] * (8 + len(edge)),
        out_specs=[VMEM] * (1 + len(edge)),
        out_shape=[pltpu.VMEM(shape, BF16)] * (1 + len(edge)),
        compiler_params=PARAMS,
        cost_estimate=pl.CostEstimate(
            flops=2 * ns * n * nc * 9 * nc,
            bytes_accessed=2 * ns * (9 * nc * nc + 7 * n * nc),
            transcendentals=0,
        ),
        name="sweep",
    )(*map(in_vmem, (*coarse, hops, dinv, *edge)))


def prolong_kernel(t, *refs):
    hops, dinv, basis, agg = refs[6:10]
    out, agg_s, value_v, out_v, sems = refs[len(refs) - 5 :]
    ns, n, nf = out_v.shape
    width = nf // PIECES
    copies = Copies(sems)
    agg_in = copies.start(agg, agg_s)
    outs = []
    for c in range(ns):
        value = next_iterate(c, *refs[:6], hops, dinv.at[t])
        if c == 0:
            value_v[c] = value
            agg_in.wait()
            value = value_v[c]
        s = (agg_s[t, 0] & 1) ^ c
        for p in range(PIECES):
            part = pl.ds(p * width, width)
            out_v[c, :, part] = lax.dot_general(
                value, basis[t, s, part], (((1,), (1,)), ((), ())), preferred_element_type=F32
            ).astype(BF16)
            outs.append(copies.start(out_v.at[c, :, part], out.at[t, s, :, part]))
    for wait in outs:
        wait.wait()


def prolong(t, shape, agg, coarse, hops, dinv, basis, previous):
    part = coarse[0].shape
    ns, n, nc = part
    nf = basis.shape[2]
    operands = [*map(in_vmem, (*coarse, hops, dinv, basis)), in_hbm(agg)]
    in_specs = [VMEM] * 9 + [HBM]
    aliases = {}
    if previous is not None:
        aliases = {len(operands): 0}
        operands.append(in_hbm(previous))
        in_specs.append(HBM)
    return pl.pallas_call(
        functools.partial(prolong_kernel, t),
        in_specs=in_specs,
        out_specs=HBM,
        out_shape=pltpu.HBM(shape, BF16),
        input_output_aliases=aliases,
        scratch_shapes=[
            pltpu.SMEM(agg.shape, jnp.int32),
            pltpu.VMEM(part, BF16),
            pltpu.VMEM((ns, n, nf), BF16),
            pltpu.SemaphoreType.DMA((1 + ns * PIECES,)),
        ],
        compiler_params=PARAMS,
        cost_estimate=pl.CostEstimate(
            flops=2 * ns * n * nc * (9 * nc + nf),
            bytes_accessed=2 * ns * (9 * nc * nc + 6 * n * nc + nf * nc + n * nf),
            transcendentals=0,
        ),
        name="prolong",
    )(*operands)


def from_next(x, axis):
    count = lax.axis_size(axis)
    return lax.ppermute(x, axis, [((i + 1) % count, i) for i in range(count)])


def from_previous(x, axis):
    count = lax.axis_size(axis)
    return lax.ppermute(x, axis, [(i, (i + 1) % count) for i in range(count)])


def swap_sites(x, offset):
    axes = ("lat", "src")
    nt, count = (lax.axis_size(a) for a in axes)
    step = lambda l, s: (s + 1 - 2 * (((l + (l < 2)) + s + offset) % 2)) % count
    pairs = [(l * count + s, l * count + step(l, s)) for l in range(nt) for s in range(count)]
    return lax.ppermute(x, axes, pairs)


def halos(e, first, last):
    spatial = [(swap_sites(x, 0), swap_sites(x, 1)) for x in e]
    beyond = from_next(first, "lat")
    before = from_previous(last, "lat")
    later = [*e[1:], beyond]
    earlier = [before, *e[:-1]]
    return [(e[t], later[t], earlier[t], *spatial[t]) for t in range(len(e))]


def body(fine, basis, dinv, hops, nbr, agg):
    slices = range(fine.shape[0])
    rhs, e, basis, dinv, hops = restrict(agg, nbr.T, fine, basis, dinv, hops)
    around = halos(e, e[0], e[-1])
    e = []
    for t in slices:
        edge = (e[0],) if t == slices[-1] else ()
        value, *edge = sweep(t, (rhs[t], *around[t]), hops[t], dinv, edge)
        e.append(value)
    around = halos(e, edge[0], e[-1])
    out = None
    for t in slices:
        out = prolong(t, fine.shape, agg, (rhs[t], *around[t]), hops[t], dinv, basis, out)
    return out


def solution(mesh):
    return jax.shard_map(
        body,
        mesh=mesh,
        in_specs=(
            P("lat", "src", None, None),
            P("lat", "src", None, None),
            P("lat", "src", None, None),
            P("lat", "src", None, None, None),
            P(),
            P("lat", "src"),
        ),
        out_specs=P("lat", "src", None, None),
        check_vma=False,
    )
```
